32 devices in a mesh: ctx: 16 (over z, y, x), tp: 2 (over core).
Axes of the slice: x: 2, y: 2, z: 4, core: 2. Of those that a mesh axis runs over, the one named last changes fastest.
Arguments:
- queries: bfloat16 [2, 2048, 4096], P(None, 'ctx', 'tp'), may hold values from -6 to 6
- key_input: bfloat16 [2, 2048, 4096], P(None, 'ctx', 'tp'), may hold values from -6 to 6
- value_input: bfloat16 [2, 2048, 4096], P(None, 'ctx', 'tp'), may hold values from -6 to 6
- filters: bfloat16 [128, 256], P(None, 'tp'), may hold values from -0.5 to 0.5
- skip_gain: float32 [4096], P('tp'), may hold values from -4 to 4
- grad_output: bfloat16 [2, 2048, 4096], P(None, 'ctx', 'tp'), may hold values from -120 to 120
Outputs:
- mixed: bfloat16 [2, 2048, 4096], P(None, 'ctx', 'tp')
- grad_queries: bfloat16 [2, 2048, 4096], P(None, 'ctx', 'tp')
- grad_keys: bfloat16 [2, 2048, 4096], P(None, 'ctx', 'tp')
- grad_values: bfloat16 [2, 2048, 4096], P(None, 'ctx', 'tp')
- filter_update: float32 [128, 256], P(None, 'tp')
- skip_update: float32 [4096], P('tp')
The draws below stay inside these ranges and needn't reach their ends.
All inputs are finite; a program needn't handle non-finite values.
Results may differ from the reference program's by a relative error of at most 0.0051.
Values may be sent and summed in bfloat16 or wider, within the bound.
A program may use at most 64 MiB of HBM per device.

```python
import jax
import jax.numpy as jnp
from jax import lax

D = 4096
NFILT = 256
FILT = 128
TOK_DEV = 128
BATCH = 2
SEQ = 2048


def draw_grad_output(key, part):
    noise_key, scale_key = jax.random.split(key, 2)
    position = jnp.arange(SEQ, dtype=jnp.float32) / max(SEQ - 1, 1)
    seq_ramp = 1.0 + 2.0 * position
    channel = jnp.arange(D, dtype=jnp.float32) / D
    spread = jax.random.uniform(scale_key, (D,), jnp.float32, -1.15, 1.15)
    scales = jnp.exp(jnp.log(3.0) * channel + spread)
    values_raw = jnp.clip(jax.random.normal(noise_key, (BATCH, SEQ, D), jnp.float32), -4.0, 4.0)
    return (values_raw * seq_ramp[None, :, None] * scales[None, None, :]).astype(jnp.bfloat16)


def block_scale(rng, extent, shards, least, largest):
    level, own = 1.0, jax.random.fold_in(rng, 6)
    for dim, blocks in shards:
        steps = jnp.exp(jax.random.uniform(jax.random.fold_in(own, dim), (blocks,), jnp.float32, least / len(shards), largest / len(shards)))
        level = level * jnp.repeat(steps, extent[dim] // blocks).reshape([-1 if axis == dim else 1 for axis in range(len(extent))])
    return level


def noise(key, shape, deviation, limit, cuts=(), kind=jnp.bfloat16):
    entries = deviation * jax.random.normal(key, shape, jnp.float32)
    if cuts:
        entries = entries * block_scale(key, shape, cuts, -0.22, 0.18)
    return jnp.clip(entries, -limit, limit).astype(kind)


def setup_inputs(seed: int = 0) -> dict:
    key_of = jax.random.split(jax.random.key(seed), 7)
    return {
        "queries": noise(key_of[0], (BATCH, SEQ, D), 1.0, 6.0, ((1, 16), (2, 2))),
        "key_input": noise(key_of[1], (BATCH, SEQ, D), 1.0, 6.0, ((1, 16), (2, 2))),
        "value_input": noise(key_of[2], (BATCH, SEQ, D), 1.0, 6.0, ((1, 16), (2, 2))),
        "filters": noise(key_of[3], (FILT, NFILT), FILT ** -0.5, 0.5, ((1, 2),)),
        "skip_gain": noise(key_of[4], (D,), 1.0, 4.0, ((0, 2),), jnp.float32),
        "grad_output": draw_grad_output(jax.random.fold_in(key_of[6], 71), 0),
    }


def toeplitz(filt, row_count):
    tap_count = filt.shape[0]
    period = row_count + tap_count
    padded = jnp.concatenate([filt[::-1], jnp.zeros((row_count, filt.shape[1]), filt.dtype)], 0)
    repeated = jnp.tile(padded, (row_count, 1))[:row_count * (period - 1)]
    return repeated.reshape(row_count, period - 1, filt.shape[1])

def rounded(values_in):
    return lax.optimization_barrier(values_in.astype(jnp.bfloat16)).astype(jnp.float32)

def banded(toeplitz_band, extended):
    filter_count = toeplitz_band.shape[2]
    ext_rows = extended.shape[0]
    grouped = extended.reshape(ext_rows, filter_count, -1)
    result = jnp.einsum('tsf,sfi->tfi', toeplitz_band, grouped, precision=lax.Precision.HIGHEST)
    return result.reshape(toeplitz_band.shape[0], -1)

def reference(queries, key_input, value_input, filters, skip_gain, grad_output):
    filters_f32 = filters.astype(jnp.float32)
    tap_count = FILT
    row_count = TOK_DEV
    filter_count = NFILT
    ext_rows = row_count + tap_count - 1
    forward_band = toeplitz(filters_f32, row_count)
    backward_band = toeplitz(filters_f32[::-1], row_count)

    def sequence_pass(items):
        query_seq = items[0].astype(jnp.float32)
        key_seq = items[1].astype(jnp.float32)
        value_seq = items[2].astype(jnp.float32)
        grad_seq = items[3].astype(jnp.float32)
        product = rounded(key_seq * value_seq)
        grad_mixer = rounded(grad_seq * query_seq)
        before = jnp.pad(product, ((tap_count - 1, 0), (0, 0)))
        later_pad = jnp.pad(grad_mixer, ((0, tap_count - 1), (0, 0)))

        def block_pass(index):
            offset = index * row_count
            ext_prod = lax.dynamic_slice_in_dim(before, offset, ext_rows, 0)
            ext_grad = lax.dynamic_slice_in_dim(later_pad, offset, ext_rows, 0)
            own_prod = lax.dynamic_slice_in_dim(product, offset, row_count, 0)
            own_grad = lax.dynamic_slice_in_dim(grad_mixer, offset, row_count, 0)
            own_query = lax.dynamic_slice_in_dim(query_seq, offset, row_count, 0)
            own_out = lax.dynamic_slice_in_dim(grad_seq, offset, row_count, 0)
            own_key = lax.dynamic_slice_in_dim(key_seq, offset, row_count, 0)
            own_value = lax.dynamic_slice_in_dim(value_seq, offset, row_count, 0)
            mixer_sum = banded(forward_band, ext_prod) + skip_gain * own_prod
            grad_product = banded(backward_band, ext_grad) + skip_gain * own_grad
            outer_sums = jnp.einsum('tfi,sfi->tsf', own_grad.reshape(row_count, filter_count, -1), ext_prod.reshape(ext_rows, filter_count, -1), precision=lax.Precision.HIGHEST)
            folded = jnp.concatenate([outer_sums.reshape(row_count * ext_rows, filter_count), jnp.zeros((row_count, filter_count), jnp.float32)], 0)
            folded = folded.reshape(row_count, ext_rows + 1, filter_count).sum(0)[:tap_count][::-1]
            return ((own_query * mixer_sum).astype(jnp.bfloat16), (own_out * mixer_sum).astype(jnp.bfloat16), (grad_product * own_value).astype(jnp.bfloat16), (grad_product * own_key).astype(jnp.bfloat16), folded, lax.optimization_barrier(jnp.sum(own_grad * own_prod, 0)))
        blocks = lax.map(block_pass, jnp.arange(SEQ // row_count, dtype=jnp.int32))
        return (blocks[0].reshape(SEQ, D), blocks[1].reshape(SEQ, D), blocks[2].reshape(SEQ, D), blocks[3].reshape(SEQ, D), lax.optimization_barrier(jnp.sum(blocks[4], 0)), lax.optimization_barrier(jnp.sum(blocks[5], 0)))
    results = lax.map(sequence_pass, (queries, key_input, value_input, grad_output))
    filter_grad = lax.optimization_barrier(jnp.sum(results[4], 0))
    skip_grad = lax.optimization_barrier(jnp.sum(results[5], 0))
    filter_update = filter_grad / jnp.sqrt(jnp.mean(filter_grad * filter_grad) + 1e-06)
    skip_update = skip_grad / jnp.sqrt(jnp.mean(skip_grad * skip_grad) + 1e-06)
    return (results[0], results[1], results[2], results[3], filter_update, skip_update)
```

```python
import functools

import jax
import jax.numpy as jnp
from jax import lax
from jax.experimental import pallas as pl
from jax.experimental.pallas import tpu as pltpu
from jax.sharding import PartitionSpec as P

MESH = pl.DeviceIdType.MESH
LANES = 128
FOLD = 16


def step_kernel(
    n,
    groups,
    in_flight,
    entries,
    filt_ref,
    skip_ref,
    q_ref,
    k_ref,
    v_ref,
    go_ref,
    mixed_ref,
    gq_ref,
    gk_ref,
    gv_ref,
    fu_ref,
    su_ref,
    prod,
    gmix,
    prod_halo,
    gmix_halo,
    fwd_rows,
    bwd_rows,
    fwd_band,
    bwd_band,
    part,
    terms,
    reduced,
    squares,
    p_send,
    p_recv,
    g_send,
    g_recv,
    rs_send,
    rs_recv,
    ag_send,
    ag_recv,
    sq_send,
    sq_recv,
):
    me = lax.axis_index("ctx")
    core = lax.axis_index("tp")
    batch, rows = q_ref.shape[0], q_ref.shape[1]
    taps = filt_ref.shape[0]
    per_group = fwd_band.shape[0] // rows
    width = LANES // per_group
    fil_entries, skip_entries = entries

    barrier = pltpu.get_barrier_semaphore()

    @pl.loop(1, n)
    def _(i):
        pl.semaphore_signal(
            barrier, inc=1, device_id=(lax.rem(me + i, n), core), device_id_type=MESH
        )

    pl.semaphore_signal(barrier, inc=1, device_id=(me, 1 - core), device_id_type=MESH)

    def p_copy(g):
        return pltpu.make_async_remote_copy(
            src_ref=prod.at[g],
            dst_ref=prod_halo.at[g],
            send_sem=p_send.at[g],
            recv_sem=p_recv.at[g],
            device_id=(lax.rem(me + 1, n), core),
            device_id_type=MESH,
        )

    def g_copy(g):
        return pltpu.make_async_remote_copy(
            src_ref=gmix.at[g],
            dst_ref=gmix_halo.at[g],
            send_sem=g_send.at[g],
            recv_sem=g_recv.at[g],
            device_id=(lax.rem(me + n - 1, n), core),
            device_id_type=MESH,
        )

    def start_halo(g):
        @pl.when(me < n - 1)
        def _():
            p_copy(g).start()

        @pl.when(me > 0)
        def _():
            g_copy(g).start()

    def lanes_of(g):
        return pl.ds(pl.multiple_of(g * LANES, LANES), LANES)

    def factors(g):
        cols = lanes_of(g)
        for b in range(batch):
            kf = k_ref[b, :, cols].astype(jnp.float32)
            vf = v_ref[b, :, cols].astype(jnp.float32)
            prod[g, b] = (kf * vf).astype(jnp.bfloat16)
            qf = q_ref[b, :, cols].astype(jnp.float32)
            of = go_ref[b, :, cols].astype(jnp.float32)
            gmix[g, b] = (qf * of).astype(jnp.bfloat16)

    factors(0)
    pl.semaphore_wait(barrier, n)
    start_halo(0)

    @pl.loop(1, groups)
    def _(g):
        factors(g)

        @pl.when(g < in_flight)
        def _():
            start_halo(g)

    @pl.when(me == 0)
    def _():
        prod_halo[...] = jnp.zeros_like(prod_halo)

    @pl.when(me == n - 1)
    def _():
        gmix_halo[...] = jnp.zeros_like(gmix_halo)

    filt_t = filt_ref[...].astype(jnp.float32).T
    src = lax.broadcasted_iota(jnp.int32, (taps, taps), 0)
    dst = lax.broadcasted_iota(jnp.int32, (taps, taps), 1)
    mirror = (lax.rem(src + dst, taps) == 0).astype(jnp.bfloat16)
    bwd_rows[...] = filt_t
    fwd_rows[...] = jnp.dot(
        filt_t.astype(jnp.bfloat16), mirror, preferred_element_type=jnp.float32
    )

    t_idx = lax.broadcasted_iota(jnp.int32, (rows, taps), 0)
    s_idx = lax.broadcasted_iota(jnp.int32, (rows, taps), 1)

    def build_bands(g):
        first = pl.ds(pl.multiple_of(g * per_group, per_group), per_group)
        fwd_taps = fwd_rows[first, :]
        bwd_taps = bwd_rows[first, :]
        for f in range(per_group):
            at = slice(f * rows, (f + 1) * rows)
            turned = pltpu.roll(
                jnp.broadcast_to(fwd_taps[f : f + 1], (rows, taps)), 0, 1, stride=1, stride_axis=0
            )
            fwd_band[at, :taps] = jnp.where(s_idx > t_idx, turned, 0.0).astype(jnp.bfloat16)
            fwd_band[at, taps:] = jnp.where(s_idx <= t_idx, turned, 0.0).astype(jnp.bfloat16)
            turned = pltpu.roll(
                jnp.broadcast_to(bwd_taps[f : f + 1], (rows, taps)), 0, 1, stride=1, stride_axis=0
            )
            bwd_band[at, :taps] = jnp.where(s_idx >= t_idx, turned, 0.0).astype(jnp.bfloat16)
            bwd_band[at, taps:] = jnp.where(s_idx < t_idx, turned, 0.0).astype(jnp.bfloat16)

    lane_filter = lax.rem(
        lax.broadcasted_iota(jnp.int32, (rows, batch * LANES), 1), LANES
    ) // width
    row_filter = lax.broadcasted_iota(jnp.int32, (rows, batch * LANES), 0) // FOLD
    own_filter = (lane_filter == row_filter).astype(jnp.float32).astype(jnp.bfloat16)

    def banded(band, ext):
        every = jnp.dot(band[...], ext, preferred_element_type=jnp.float32)
        picked = every[:rows]
        for f in range(1, per_group):
            picked = jnp.where(lane_filter == f, every[f * rows : (f + 1) * rows], picked)
        return picked

    @pl.loop(0, groups)
    def _(g):
        cols = lanes_of(g)
        build_bands(g)

        @pl.when(me > 0)
        def _():
            p_copy(g).wait_recv()

        @pl.when(me < n - 1)
        def _():
            g_copy(g).wait_recv()

        @pl.when(g + in_flight < groups)
        def _():
            start_halo(g + in_flight)

        gain = skip_ref[pl.ds(g, 1), :]
        own_p = [prod[g, b] for b in range(batch)]
        own_g = [gmix[g, b] for b in range(batch)]
        ext_p = jnp.concatenate(
            [jnp.concatenate([prod_halo[g, b] for b in range(batch)], 1), jnp.concatenate(own_p, 1)], 0
        )
        ext_g = jnp.concatenate(
            [jnp.concatenate(own_g, 1), jnp.concatenate([gmix_halo[g, b] for b in range(batch)], 1)], 0
        )
        forward = banded(fwd_band, ext_p)
        backward = banded(bwd_band, ext_g)
        skip_sum = jnp.zeros((1, LANES), jnp.float32)
        for b in range(batch):
            pf = own_p[b].astype(jnp.float32)
            gf = own_g[b].astype(jnp.float32)
            at = slice(b * LANES, (b + 1) * LANES)
            mixer = forward[:, at] + gain * pf
            grad_p = backward[:, at] + gain * gf
            mixed_ref[b, :, cols] = (q_ref[b, :, cols].astype(jnp.float32) * mixer).astype(jnp.bfloat16)
            gq_ref[b, :, cols] = (go_ref[b, :, cols].astype(jnp.float32) * mixer).astype(jnp.bfloat16)
            gk_ref[b, :, cols] = (v_ref[b, :, cols].astype(jnp.float32) * grad_p).astype(jnp.bfloat16)
            gv_ref[b, :, cols] = (k_ref[b, :, cols].astype(jnp.float32) * grad_p).astype(jnp.bfloat16)
            skip_sum = skip_sum + jnp.sum(pf * gf, axis=0, keepdims=True)

        wide_p = jnp.concatenate(own_p, 1)
        lhs, rhs = [], []
        blank = jnp.zeros((2 * taps - taps - FOLD, batch * LANES), jnp.bfloat16)
        for a in range(rows // FOLD):
            piece = wide_p[a * FOLD : (a + 1) * FOLD]
            lhs.append(jnp.concatenate([piece] * per_group, 0) * own_filter)
            rhs.append(jnp.concatenate([ext_g[a * FOLD : a * FOLD + taps + FOLD], blank], 0))
        outer = lax.dot_general(
            jnp.concatenate(lhs, 1),
            jnp.concatenate(rhs, 1),
            (((1,), (1,)), ((), ())),
            preferred_element_type=jnp.float32,
        )
        span = outer.shape[1]
        halves = outer.reshape(per_group, 2, FOLD // 2, span)
        upper = halves[:, 0].reshape(per_group * FOLD // 2, span)
        lower = halves[:, 1].reshape(per_group * FOLD // 2, span)
        summed = upper + pltpu.roll(lower, span - FOLD // 2, 1)
        row_of = lax.rem(
            lax.broadcasted_iota(jnp.int32, summed.shape, 0), FOLD // 2
        )
        for bit in (4, 2, 1):
            summed = jnp.where(
                lax.rem(row_of // bit, 2) == 1, pltpu.roll(summed, span - bit, 1), summed
            )
        tap_sums = jnp.sum(summed.reshape(per_group, FOLD // 2, span), axis=1)
        part[g, :per_group, :] = tap_sums[:, :taps]
        part[g, per_group:, :] = jnp.broadcast_to(skip_sum, (part.shape[1] - per_group, LANES))

        @pl.when(me == g)
        def _():
            terms[n - 1] = part[g]

        @pl.when(me != g)
        def _():
            pltpu.make_async_remote_copy(
                src_ref=part.at[g],
                dst_ref=terms.at[lax.rem(me - g - 1 + n, n)],
                send_sem=rs_send,
                recv_sem=rs_recv,
                device_id=(g, core),
                device_id_type=MESH,
            ).start()

    def wait_bytes(buffer, count, sem):
        pltpu.make_async_copy(buffer.at[pl.ds(0, count)], buffer.at[pl.ds(0, count)], sem).wait()

    @pl.when(me < groups)
    def _():
        wait_bytes(terms, n - 1, rs_recv)
        total = terms[0]
        for i in range(1, n):
            total = total + terms[i]
        reduced[me] = total

        @pl.loop(1, n)
        def _(i):
            pltpu.make_async_remote_copy(
                src_ref=reduced.at[me],
                dst_ref=reduced.at[me],
                send_sem=ag_send,
                recv_sem=ag_recv,
                device_id=(lax.rem(me + i, n), core),
                device_id_type=MESH,
            ).start()

        wait_bytes(reduced, groups - 1, ag_recv)

    @pl.when(me >= groups)
    def _():
        wait_bytes(reduced, groups, ag_recv)

    fil = reduced[:, :per_group, :].reshape(groups * per_group, taps)
    skp = reduced[:, per_group, :]
    squares[0, 0:8, :] = jnp.sum((fil * fil).reshape(groups, per_group, taps), axis=0)
    squares[0, 8:16, :] = jnp.sum((skp * skp).reshape(groups // 8, 8, LANES), axis=0)
    swap = pltpu.make_async_remote_copy(
        src_ref=squares.at[0],
        dst_ref=squares.at[1],
        send_sem=sq_send,
        recv_sem=sq_recv,
        device_id=(me, 1 - core),
        device_id_type=MESH,
    )
    swap.start()
    fil_t = fil.T
    swap.wait()
    both = squares[0] + squares[1]
    fil_mean = jnp.sum(both[0:8]) / fil_entries
    skip_mean = jnp.sum(both[8:16]) / skip_entries
    fu_ref[...] = fil_t / jnp.sqrt(jnp.full(fil_t.shape, fil_mean, jnp.float32) + 1e-06)
    su_ref[...] = skp / jnp.sqrt(jnp.full(skp.shape, skip_mean, jnp.float32) + 1e-06)

    @pl.loop(0, groups)
    def _(g):
        @pl.when(me < n - 1)
        def _():
            p_copy(g).wait_send()

        @pl.when(me > 0)
        def _():
            g_copy(g).wait_send()

    @pl.when(me < groups)
    def _():
        wait_bytes(part, groups - 1, rs_send)
        wait_bytes(terms, n - 1, ag_send)

    @pl.when(me >= groups)
    def _():
        wait_bytes(part, groups, rs_send)


def on_device(in_flight, queries, key_input, value_input, filters, skip_gain, grad_output):
    batch, rows, channels = queries.shape
    taps, filter_count = filters.shape
    groups = channels // LANES
    per_group = filter_count // groups
    n = lax.axis_size("ctx")
    cores = lax.axis_size("tp")
    entries = (float(taps * filter_count * cores), float(channels * cores))
    vmem = pl.BlockSpec(memory_space=pltpu.VMEM)
    chunk = (groups, batch, rows, LANES)
    act = jax.ShapeDtypeStruct(queries.shape, jnp.bfloat16)
    outs = pl.pallas_call(
        functools.partial(step_kernel, n, groups, in_flight, entries),
        out_shape=(
            act,
            act,
            act,
            act,
            jax.ShapeDtypeStruct((taps, filter_count), jnp.float32),
            jax.ShapeDtypeStruct((groups, LANES), jnp.float32),
        ),
        in_specs=[vmem] * 6,
        out_specs=(vmem,) * 6,
        scratch_shapes=[
            pltpu.VMEM(chunk, jnp.bfloat16),
            pltpu.VMEM(chunk, jnp.bfloat16),
            pltpu.VMEM(chunk, jnp.bfloat16),
            pltpu.VMEM(chunk, jnp.bfloat16),
            pltpu.VMEM((filter_count, taps), jnp.float32),
            pltpu.VMEM((filter_count, taps), jnp.float32),
            pltpu.VMEM((per_group * rows, 2 * taps), jnp.bfloat16),
            pltpu.VMEM((per_group * rows, 2 * taps), jnp.bfloat16),
            pltpu.VMEM((groups, 16, LANES), jnp.float32),
            pltpu.VMEM((n, 16, LANES), jnp.float32),
            pltpu.VMEM((groups, 16, LANES), jnp.float32),
            pltpu.VMEM((2, 16, LANES), jnp.float32),
            pltpu.SemaphoreType.DMA((groups,)),
            pltpu.SemaphoreType.DMA((groups,)),
            pltpu.SemaphoreType.DMA((groups,)),
            pltpu.SemaphoreType.DMA((groups,)),
            pltpu.SemaphoreType.DMA,
            pltpu.SemaphoreType.DMA,
            pltpu.SemaphoreType.DMA,
            pltpu.SemaphoreType.DMA,
            pltpu.SemaphoreType.DMA,
            pltpu.SemaphoreType.DMA,
        ],
        compiler_params=pltpu.CompilerParams(
            collective_id=0, has_side_effects=True, vmem_limit_bytes=48 * 1024 * 1024
        ),
    )(filters, skip_gain.reshape(groups, LANES), queries, key_input, value_input, grad_output)
    return (*outs[:5], outs[5].reshape(channels))


def solution(mesh):
    act = P(None, "ctx", "tp")
    return jax.shard_map(
        functools.partial(on_device, 16),
        mesh=mesh,
        in_specs=(act, act, act, P(None, "tp"), P("tp"), act),
        out_specs=(act, act, act, act, P(None, "tp"), P("tp")),
        check_vma=False,
    )
```

```python
import functools

import jax
import jax.numpy as jnp
from jax import lax
from jax.experimental import pallas as pl
from jax.experimental.pallas import tpu as pltpu
from jax.sharding import PartitionSpec as P

MESH = pl.DeviceIdType.MESH
LANES = 128
FOLD = 16
LOADS = 4
AHEAD = 4


def step_kernel(
    n,
    groups,
    entries,
    filt_ref,
    skip_ref,
    q_hbm,
    k_hbm,
    v_hbm,
    go_hbm,
    mixed_ref,
    gq_ref,
    gk_ref,
    gv_ref,
    fu_ref,
    su_ref,
    q_ref,
    k_ref,
    v_ref,
    go_ref,
    prod,
    gmix,
    prod_halo,
    gmix_halo,
    fwd_rows,
    bwd_rows,
    fwd_band,
    bwd_band,
    part,
    terms,
    reduced,
    squares,
    in_sem,
    p_send,
    p_recv,
    g_send,
    g_recv,
    rs_send,
    rs_recv,
    ag_send,
    ag_recv,
    sq_send,
    sq_recv,
):
    me = lax.axis_index("ctx")
    core = lax.axis_index("tp")
    batch, rows = q_ref.shape[0], q_ref.shape[1]
    taps = filt_ref.shape[0]
    per_group = fwd_band.shape[0] // rows
    width = LANES // per_group
    fil_entries, skip_entries = entries

    wide = q_hbm.shape[2] // LOADS
    sources = ((q_hbm, q_ref), (go_hbm, go_ref), (k_hbm, k_ref), (v_hbm, v_ref))

    def load(array, part_of):
        src, dst = sources[array]
        at = pl.ds(part_of * wide, wide)
        return pltpu.make_async_copy(src.at[:, :, at], dst.at[:, :, at], in_sem.at[array, part_of])

    for first in (0, 2):
        for c in range(LOADS):
            load(first, c).start()
            load(first + 1, c).start()

    barrier = pltpu.get_barrier_semaphore()

    @pl.loop(1, n)
    def _(i):
        pl.semaphore_signal(
            barrier, inc=1, device_id=(lax.rem(me + i, n), core), device_id_type=MESH
        )

    pl.semaphore_signal(barrier, inc=1, device_id=(me, 1 - core), device_id_type=MESH)

    def p_copy(g):
        return pltpu.make_async_remote_copy(
            src_ref=prod.at[g],
            dst_ref=prod_halo.at[g],
            send_sem=p_send.at[g],
            recv_sem=p_recv.at[g],
            device_id=(lax.rem(me + 1, n), core),
            device_id_type=MESH,
        )

    def g_copy(g):
        return pltpu.make_async_remote_copy(
            src_ref=gmix.at[g],
            dst_ref=gmix_halo.at[g],
            send_sem=g_send.at[g],
            recv_sem=g_recv.at[g],
            device_id=(lax.rem(me + n - 1, n), core),
            device_id_type=MESH,
        )

    def lanes_of(g):
        return pl.ds(pl.multiple_of(g * LANES, LANES), LANES)

    def times(out, left, right, g):
        cols = lanes_of(g)
        for b in range(batch):
            lf = left[b, :, cols].astype(jnp.float32)
            rf = right[b, :, cols].astype(jnp.float32)
            out[g, b] = (lf * rf).astype(jnp.bfloat16)

    per_load = groups // LOADS
    for c in range(LOADS):
        load(0, c).wait()
        load(1, c).wait()
        if c == 0:
            pl.semaphore_wait(barrier, n)

        @pl.loop(c * per_load, (c + 1) * per_load)
        def _(g):
            times(gmix, q_ref, go_ref, g)

            @pl.when(me > 0)
            def _():
                g_copy(g).start()

    for c in range(LOADS):
        load(2, c).wait()
        load(3, c).wait()

        @pl.loop(c * per_load, (c + 1) * per_load)
        def _(g):
            times(prod, k_ref, v_ref, g)

    @pl.when(me == 0)
    def _():
        prod_halo[...] = jnp.zeros_like(prod_halo)

    @pl.when(me == n - 1)
    def _():
        gmix_halo[...] = jnp.zeros_like(gmix_halo)

    filt_t = filt_ref[...].astype(jnp.float32).T
    src = lax.broadcasted_iota(jnp.int32, (taps, taps), 0)
    dst = lax.broadcasted_iota(jnp.int32, (taps, taps), 1)
    mirror = (lax.rem(src + dst, taps) == 0).astype(jnp.bfloat16)
    bwd_rows[...] = filt_t
    fwd_rows[...] = jnp.dot(
        filt_t.astype(jnp.bfloat16), mirror, preferred_element_type=jnp.float32
    )

    t_idx = lax.broadcasted_iota(jnp.int32, (rows, taps), 0)
    s_idx = lax.broadcasted_iota(jnp.int32, (rows, taps), 1)

    def build_band(band, tap_rows, g, left, right):
        own = tap_rows[pl.ds(pl.multiple_of(g * per_group, per_group), per_group), :]
        for f in range(per_group):
            at = slice(f * rows, (f + 1) * rows)
            turned = pltpu.roll(
                jnp.broadcast_to(own[f : f + 1], (rows, taps)), 0, 1, stride=1, stride_axis=0
            )
            band[at, :taps] = jnp.where(left, turned, 0.0).astype(jnp.bfloat16)
            band[at, taps:] = jnp.where(right, turned, 0.0).astype(jnp.bfloat16)

    lane_filter = lax.rem(
        lax.broadcasted_iota(jnp.int32, (rows, batch * LANES), 1), LANES
    ) // width
    row_filter = lax.broadcasted_iota(jnp.int32, (rows, batch * LANES), 0) // FOLD
    own_filter = (lane_filter == row_filter).astype(jnp.float32).astype(jnp.bfloat16)

    def banded(band, ext):
        every = jnp.dot(band[...], ext, preferred_element_type=jnp.float32)
        picked = every[:rows]
        for f in range(1, per_group):
            picked = jnp.where(lane_filter == f, every[f * rows : (f + 1) * rows], picked)
        return picked

    def send_product(g):
        @pl.when(me < n - 1)
        def _():
            p_copy(g).start()

    def forward_step(g):
        cols = lanes_of(g)
        build_band(fwd_band, fwd_rows, g, s_idx > t_idx, s_idx <= t_idx)

        @pl.when(me > 0)
        def _():
            p_copy(g).wait_recv()

        @pl.when(g + AHEAD < groups)
        def _():
            send_product(g + AHEAD)

        gain = skip_ref[pl.ds(g, 1), :]
        own_p = [prod[g, b] for b in range(batch)]
        ext_p = jnp.concatenate(
            [jnp.concatenate([prod_halo[g, b] for b in range(batch)], 1), jnp.concatenate(own_p, 1)], 0
        )
        forward = banded(fwd_band, ext_p)
        for b in range(batch):
            at = slice(b * LANES, (b + 1) * LANES)
            mixer = forward[:, at] + gain * own_p[b].astype(jnp.float32)
            mixed_ref[b, :, cols] = (q_ref[b, :, cols].astype(jnp.float32) * mixer).astype(jnp.bfloat16)
            gq_ref[b, :, cols] = (go_ref[b, :, cols].astype(jnp.float32) * mixer).astype(jnp.bfloat16)

    @pl.loop(0, groups)
    def _(g):
        cols = lanes_of(g)
        build_band(bwd_band, bwd_rows, g, s_idx >= t_idx, s_idx < t_idx)

        @pl.when(me < n - 1)
        def _():
            g_copy(g).wait_recv()

        @pl.when(g >= groups - AHEAD)
        def _():
            send_product(g + AHEAD - groups)

        gain = skip_ref[pl.ds(g, 1), :]
        own_p = [prod[g, b] for b in range(batch)]
        own_g = [gmix[g, b] for b in range(batch)]
        ext_g = jnp.concatenate(
            [jnp.concatenate(own_g, 1), jnp.concatenate([gmix_halo[g, b] for b in range(batch)], 1)], 0
        )
        backward = banded(bwd_band, ext_g)
        skip_sum = jnp.zeros((1, LANES), jnp.float32)
        for b in range(batch):
            pf = own_p[b].astype(jnp.float32)
            gf = own_g[b].astype(jnp.float32)
            at = slice(b * LANES, (b + 1) * LANES)
            grad_p = backward[:, at] + gain * gf
            gk_ref[b, :, cols] = (v_ref[b, :, cols].astype(jnp.float32) * grad_p).astype(jnp.bfloat16)
            gv_ref[b, :, cols] = (k_ref[b, :, cols].astype(jnp.float32) * grad_p).astype(jnp.bfloat16)
            skip_sum = skip_sum + jnp.sum(pf * gf, axis=0, keepdims=True)

        wide_p = jnp.concatenate(own_p, 1)
        lhs, rhs = [], []
        blank = jnp.zeros((2 * taps - taps - FOLD, batch * LANES), jnp.bfloat16)
        for a in range(rows // FOLD):
            piece = wide_p[a * FOLD : (a + 1) * FOLD]
            lhs.append(jnp.concatenate([piece] * per_group, 0) * own_filter)
            rhs.append(jnp.concatenate([ext_g[a * FOLD : a * FOLD + taps + FOLD], blank], 0))
        outer = lax.dot_general(
            jnp.concatenate(lhs, 1),
            jnp.concatenate(rhs, 1),
            (((1,), (1,)), ((), ())),
            preferred_element_type=jnp.float32,
        )
        span = outer.shape[1]
        halves = outer.reshape(per_group, 2, FOLD // 2, span)
        upper = halves[:, 0].reshape(per_group * FOLD // 2, span)
        lower = halves[:, 1].reshape(per_group * FOLD // 2, span)
        summed = upper + pltpu.roll(lower, span - FOLD // 2, 1)
        row_of = lax.rem(
            lax.broadcasted_iota(jnp.int32, summed.shape, 0), FOLD // 2
        )
        for bit in (4, 2, 1):
            summed = jnp.where(
                lax.rem(row_of // bit, 2) == 1, pltpu.roll(summed, span - bit, 1), summed
            )
        tap_sums = jnp.sum(summed.reshape(per_group, FOLD // 2, span), axis=1)
        part[g, :per_group, :] = tap_sums[:, :taps]
        part[g, per_group:, :] = jnp.broadcast_to(skip_sum, (part.shape[1] - per_group, LANES))

        @pl.when(me == g)
        def _():
            terms[n - 1] = part[g]

        @pl.when(me != g)
        def _():
            pltpu.make_async_remote_copy(
                src_ref=part.at[g],
                dst_ref=terms.at[lax.rem(me - g - 1 + n, n)],
                send_sem=rs_send,
                recv_sem=rs_recv,
                device_id=(g, core),
                device_id_type=MESH,
            ).start()

    def wait_bytes(buffer, count, sem):
        pltpu.make_async_copy(buffer.at[pl.ds(0, count)], buffer.at[pl.ds(0, count)], sem).wait()

    pl.loop(0, groups // 4)(forward_step)

    @pl.when(me < groups)
    def _():
        wait_bytes(terms, n - 1, rs_recv)
        total = terms[0]
        for i in range(1, n):
            total = total + terms[i]
        reduced[me] = total

        @pl.loop(1, n)
        def _(i):
            pltpu.make_async_remote_copy(
                src_ref=reduced.at[me],
                dst_ref=reduced.at[me],
                send_sem=ag_send,
                recv_sem=ag_recv,
                device_id=(lax.rem(me + i, n), core),
                device_id_type=MESH,
            ).start()

    pl.loop(groups // 4, groups // 2)(forward_step)

    @pl.when(me < groups)
    def _():
        wait_bytes(reduced, groups - 1, ag_recv)

    @pl.when(me >= groups)
    def _():
        wait_bytes(reduced, groups, ag_recv)

    fil = reduced[:, :per_group, :].reshape(groups * per_group, taps)
    skp = reduced[:, per_group, :]
    squares[0, 0:8, :] = jnp.sum((fil * fil).reshape(groups, per_group, taps), axis=0)
    squares[0, 8:16, :] = jnp.sum((skp * skp).reshape(groups // 8, 8, LANES), axis=0)
    swap = pltpu.make_async_remote_copy(
        src_ref=squares.at[0],
        dst_ref=squares.at[1],
        send_sem=sq_send,
        recv_sem=sq_recv,
        device_id=(me, 1 - core),
        device_id_type=MESH,
    )
    swap.start()
    pl.loop(groups // 2, groups * 3 // 4)(forward_step)
    fil_t = reduced[:, :per_group, :].reshape(groups * per_group, taps).T
    skp = reduced[:, per_group, :]
    swap.wait()
    both = squares[0] + squares[1]
    fil_mean = jnp.sum(both[0:8]) / fil_entries
    skip_mean = jnp.sum(both[8:16]) / skip_entries
    fu_ref[...] = fil_t / jnp.sqrt(jnp.full(fil_t.shape, fil_mean, jnp.float32) + 1e-06)
    su_ref[...] = skp / jnp.sqrt(jnp.full(skp.shape, skip_mean, jnp.float32) + 1e-06)

    pl.loop(groups * 3 // 4, groups)(forward_step)

    @pl.loop(0, groups)
    def _(g):
        @pl.when(me < n - 1)
        def _():
            p_copy(g).wait_send()

        @pl.when(me > 0)
        def _():
            g_copy(g).wait_send()

    @pl.when(me < groups)
    def _():
        wait_bytes(part, groups - 1, rs_send)
        wait_bytes(terms, n - 1, ag_send)

    @pl.when(me >= groups)
    def _():
        wait_bytes(part, groups, rs_send)


def on_device(queries, key_input, value_input, filters, skip_gain, grad_output):
    batch, rows, channels = queries.shape
    taps, filter_count = filters.shape
    groups = channels // LANES
    per_group = filter_count // groups
    n = lax.axis_size("ctx")
    cores = lax.axis_size("tp")
    entries = (float(taps * filter_count * cores), float(channels * cores))
    vmem = pl.BlockSpec(memory_space=pltpu.VMEM)
    hbm = pl.BlockSpec(memory_space=pltpu.HBM)
    chunk = (groups, batch, rows, LANES)
    act = jax.ShapeDtypeStruct(queries.shape, jnp.bfloat16)
    outs = pl.pallas_call(
        functools.partial(step_kernel, n, groups, entries),
        out_shape=(
            act,
            act,
            act,
            act,
            jax.ShapeDtypeStruct((taps, filter_count), jnp.float32),
            jax.ShapeDtypeStruct((groups, LANES), jnp.float32),
        ),
        in_specs=[vmem] * 2 + [hbm] * 4,
        out_specs=(vmem,) * 6,
        scratch_shapes=[pltpu.VMEM(queries.shape, jnp.bfloat16)] * 4
        + [
            pltpu.VMEM(chunk, jnp.bfloat16),
            pltpu.VMEM(chunk, jnp.bfloat16),
            pltpu.VMEM(chunk, jnp.bfloat16),
            pltpu.VMEM(chunk, jnp.bfloat16),
            pltpu.VMEM((filter_count, taps), jnp.float32),
            pltpu.VMEM((filter_count, taps), jnp.float32),
            pltpu.VMEM((per_group * rows, 2 * taps), jnp.bfloat16),
            pltpu.VMEM((per_group * rows, 2 * taps), jnp.bfloat16),
            pltpu.VMEM((groups, 16, LANES), jnp.float32),
            pltpu.VMEM((n, 16, LANES), jnp.float32),
            pltpu.VMEM((groups, 16, LANES), jnp.float32),
            pltpu.VMEM((2, 16, LANES), jnp.float32),
            pltpu.SemaphoreType.DMA((4, LOADS)),
            pltpu.SemaphoreType.DMA((groups,)),
            pltpu.SemaphoreType.DMA((groups,)),
            pltpu.SemaphoreType.DMA((groups,)),
            pltpu.SemaphoreType.DMA((groups,)),
            pltpu.SemaphoreType.DMA,
            pltpu.SemaphoreType.DMA,
            pltpu.SemaphoreType.DMA,
            pltpu.SemaphoreType.DMA,
            pltpu.SemaphoreType.DMA,
            pltpu.SemaphoreType.DMA,
        ],
        compiler_params=pltpu.CompilerParams(
            collective_id=0, has_side_effects=True, vmem_limit_bytes=49 * 1024 * 1024
        ),
    )(filters, skip_gain.reshape(groups, LANES), queries, key_input, value_input, grad_output)
    return (*outs[:5], outs[5].reshape(channels))


def solution(mesh):
    act = P(None, "ctx", "tp")
    return jax.shard_map(
        on_device,
        mesh=mesh,
        in_specs=(act, act, act, P(None, "tp"), P("tp"), act),
        out_specs=(act, act, act, act, P(None, "tp"), P("tp")),
        check_vma=False,
    )
```
